256 devices in a mesh: grow: 64 (over y, x_hi, z), lat: 4 (over x_lo, core).
Axes of the slice: x: 4 (x_hi: 2, x_lo: 2; x = x_hi * 2 + x_lo), y: 4, z: 8, core: 2. Of those that a mesh axis runs over, the one named last changes fastest.
Arguments:
- labels: int32 [1024, 128, 128], P('grow', 'lat'), may hold values from 0 to 3
- roughness: float32 [4, 1024, 128, 128], P(None, 'grow', 'lat'), may hold values from 0.1 to 1
- potential: float32 [2, 1024, 128, 128], P(None, 'grow', 'lat'), may hold values from -3 to 3
- grad_coef: float32 [4, 3], replicated, may hold values from 0.2 to 1
- composition: float32 [4, 2], replicated, may hold values from -2 to 2
- latent: float32 [4], replicated, may hold values from 0.5 to 2
- diffusivity: float32 [2], replicated, may hold values from 0.5 to 2
- melt_table: float32 [16, 2], replicated, may hold values from -1 to 1
- melt_index: int32 [4, 8, 128, 128], P(None, None, 'lat'), may hold values from 0 to 15
Outputs:
- phases: float32 [4, 1024, 128, 128], P(None, 'grow', 'lat')
- potentials: float32 [2, 1024, 128, 128], P(None, 'grow', 'lat')
The draws below stay inside these ranges and needn't reach their ends.
All inputs are finite; a program needn't handle non-finite values.
Results may differ from the reference program's by a relative error of at most 0.00025.
Values sent between devices are 32-bit elements; how exact they have to be, the bound alone decides.
A program may use at most 64 MiB of HBM per device.

```python
import math
import jax
import jax.numpy as jnp

NY = 128
STEPS = 4
ROUNDS = 4
SHIFT = 8
MELT = 16
NG = 1024
NX = 128


def plant(entries, key, low, largest):
    index_at = [jax.random.randint(jax.random.fold_in(key, axis), (), 0, length) for axis, length in enumerate(entries.shape)]
    longest = entries.shape.index(max(entries.shape))
    beside = index_at[:longest] + [(index_at[longest] + 1) % entries.shape[longest]] + index_at[longest + 1:]
    return entries.at[tuple(index_at)].set(low).at[tuple(beside)].set(largest)


def level_of(own_key, dims, pieces, low, high):
    def one(axis_at, shards_of):
        draws = jax.random.uniform(jax.random.fold_in(jax.random.fold_in(own_key, 6), axis_at), (shards_of,), jnp.float32, low / len(pieces), high / len(pieces))
        return jnp.repeat(jnp.exp(draws), dims[axis_at] // shards_of).reshape((-1,) + (1,) * (len(dims) - axis_at - 1))

    gain = one(*pieces[0])
    for cut in pieces[1:]:
        gain = gain * one(*cut)
    return gain


def bell_draw(own_key, shape, spread, most, pieces=(), kind=jnp.bfloat16):
    array = spread * jax.random.normal(own_key, shape, jnp.float32)
    if pieces:
        array = array * level_of(own_key, shape, pieces, -0.22, 0.18)
    return jnp.clip(array, -most, most).astype(kind)


def setup_inputs(seed: int = 0) -> dict:
    splits = jax.random.split(jax.random.key(seed), 10)
    labels = plant(jax.random.randint(splits[0], (NG, NX, NY), 0, 4), jax.random.fold_in(splits[0], 1), 0, 3).astype(jnp.int32)
    roughness = jnp.clip(jnp.exp(math.log(1.0) - 2.3025851 * jax.random.uniform(splits[1], (4, NG, NX, NY), jnp.float32) ** level_of(splits[1], (4, NG, NX, NY), ((1, 64), (2, 4)), -0.2, 0.2)), 0.1, 1.0)
    potential = bell_draw(splits[2], (2, NG, NX, NY), 0.5, 3.0, ((1, 64), (2, 4)), jnp.float32)
    grad_coef = jnp.clip(jnp.exp(jax.random.uniform(splits[3], (4, 3), jnp.float32, math.log(0.2), math.log(1.0))), 0.2, 1.0)
    composition = bell_draw(splits[4], (4, 2), 0.5, 2.0, (), jnp.float32)
    latent = jnp.clip(jax.random.uniform(splits[5], (4,), jnp.float32, 0.5, 2.0), 0.5, 2.0)
    diffusivity = jnp.clip(jnp.exp(jax.random.uniform(splits[6], (2,), jnp.float32, math.log(0.5), math.log(2.0))), 0.5, 2.0)
    melt_table = jnp.clip(jax.random.uniform(splits[7], (MELT, 2), jnp.float32, -1.0, 1.0), -1.0, 1.0)
    melt_index = plant(jax.random.randint(splits[8], (ROUNDS, SHIFT, NX, NY), 0, MELT), jax.random.fold_in(splits[8], 1), 0, MELT - 1).astype(jnp.int32)
    return {"labels": labels, "roughness": roughness, "potential": potential, "grad_coef": grad_coef, "composition": composition, "latent": latent, "diffusivity": diffusivity, "melt_table": melt_table, "melt_index": melt_index}


def advance(padded, grad_coef, composition, latent, diffusivity, first, total):
    center = padded[:, 1:-1, 1:-1]
    gsum = padded[:, 2:, 1:-1] + padded[:, :-2, 1:-1] - 2.0 * center
    xsum = padded[:, 1:-1, 2:] + padded[:, 1:-1, :-2] - 2.0 * center
    ysum = jnp.roll(center, 1, 3) + jnp.roll(center, -1, 3) - 2.0 * center
    fracs = center[:4]
    chem = center[4:]
    lap_phi = (grad_coef[:, 0][:, None, None, None] * gsum[:4]
               + grad_coef[:, 1][:, None, None, None] * xsum[:4]
               + grad_coef[:, 2][:, None, None, None] * ysum[:4])
    lap_mu = gsum[4:] + xsum[4:] + ysum[4:]
    rows = center.shape[1]
    theta = ((jnp.arange(rows, dtype=jnp.int32) + first).astype(jnp.float32) - 0.5 * total) / total
    psi = (composition[:, 0][:, None, None, None] * chem[0]
           + composition[:, 1][:, None, None, None] * chem[1]
           + latent[:, None, None, None] * theta[None, :, None, None])
    summed = jnp.sum(fracs, axis=0)
    rhs = lap_phi - 1.0 * (summed[None] - fracs) - psi
    rhs = rhs - jnp.mean(rhs, axis=0)[None]
    trial = fracs + 0.04 * rhs
    clipped = jnp.clip(trial, 0.0, 1.0)
    newphi = clipped / jnp.sum(clipped, axis=0)[None]
    change = newphi - fracs
    release = jnp.stack([jnp.sum(composition[:, 0][:, None, None, None] * change, axis=0),
                         jnp.sum(composition[:, 1][:, None, None, None] * change, axis=0)])
    newmu = chem + 0.04 * diffusivity[:, None, None, None] * lap_mu - release
    return jnp.concatenate([newphi, newmu], axis=0)


def reference(labels, roughness, potential, grad_coef, composition, latent, diffusivity, melt_table, melt_index):
    ngrid = labels.shape[0]
    kinds = jnp.arange(4, dtype=jnp.int32)[:, None, None, None]
    onehot = (labels[None] == kinds).astype(jnp.float32)
    fracs = (3.0 * onehot + roughness) / (3.0 + jnp.sum(roughness, axis=0))[None]
    state = jnp.concatenate([fracs, potential], axis=0)
    total = float(ngrid)
    for turn in range(ROUNDS):
        for step in range(STEPS):
            padded = jnp.pad(state, ((0, 0), (1, 1), (0, 0), (0, 0)), mode="edge")
            padded = jnp.concatenate([padded[:, :, -1:], padded, padded[:, :, :1]], axis=2)
            state = advance(padded, grad_coef, composition, latent, diffusivity, SHIFT * turn, total)
        chosen = melt_index[turn]
        melt_mu = jnp.moveaxis(melt_table[chosen], -1, 0)
        zeros = jnp.zeros(chosen.shape, jnp.float32)
        fresh = jnp.concatenate([jnp.stack([zeros, zeros, zeros, zeros + 1.0]), melt_mu], axis=0)
        state = jnp.concatenate([state[:, SHIFT:], fresh], axis=1)
    return state[:4], state[4:]
```

```python
import functools

import jax
import jax.numpy as jnp
from jax import lax
from jax.experimental import pallas as pl
from jax.experimental.pallas import tpu as pltpu
from jax.sharding import PartitionSpec as P

MESH = pl.DeviceIdType.MESH
STEPS = 4
ROUNDS = 4
SHIFT = 8
DT = 0.04
TOTAL = STEPS * ROUNDS
FIELDS = 5
PAD = 8
AHEAD = 2
HIGH = 16


def kernel(
    peers,
    lats,
    labels,
    rough,
    pot,
    melt_index,
    grad,
    comp,
    latent,
    diff,
    table,
    phases,
    potentials,
    own,
    state,
    odd,
    even,
    z_send,
    z_recv,
    x_send,
    x_recv,
):
    block, rows, cols = labels.shape
    stream = block + 2 * TOTAL
    halo = TOTAL
    low = PAD + halo
    high = low + rows
    planes = peers * block
    p = lax.axis_index("grow")
    q = lax.axis_index("lat")
    below = jnp.maximum(p - 1, 0)
    above = jnp.minimum(p + 1, peers - 1)
    left = lax.rem(q + lats - 1, lats)
    right = lax.rem(q + 1, lats)

    barrier = pltpu.get_barrier_semaphore()
    for side in (left, right):
        pl.semaphore_signal(barrier, inc=1, device_id=(p, side), device_id_type=MESH)

    @pl.when(p < peers - 1)
    def _():
        pl.semaphore_signal(barrier, inc=1, device_id=(above, q), device_id_type=MESH)

    def begin(i, carry):
        label = labels[i]
        parts = [rough[a, i] for a in range(4)]
        scale = 1.0 / (3.0 + (parts[0] + parts[1] + parts[2] + parts[3]))
        for a in range(3):
            own[i, a] = (jnp.where(label == a, 3.0, 0.0) + parts[a]) * scale
        for k in range(2):
            own[i, 3 + k] = pot[k, i]
        return carry

    lax.fori_loop(0, block, begin, 0)

    @pl.when(p == peers - 1)
    def _():
        def melt(j, carry):
            chosen = melt_index[j // SHIFT, lax.rem(j, SHIFT)]
            zero = jnp.zeros((rows, cols), jnp.float32)
            for a in range(3):
                state[j, a, pl.ds(low, rows)] = zero
            for k in range(2):
                value = zero + table[0, k]
                for e in range(1, table.shape[0]):
                    value = jnp.where(chosen == e, table[e, k], value)
                state[j, 3 + k, pl.ds(low, rows)] = value
            return carry

        lax.fori_loop(0, ROUNDS * SHIFT, melt, 0)

        def beyond(j, carry):
            for f in range(FIELDS):
                state[j, f, pl.ds(low, rows)] = jnp.zeros((rows, cols), jnp.float32)
            return carry

        lax.fori_loop(ROUNDS * SHIFT, stream, beyond, 0)

    pl.semaphore_wait(barrier, jnp.where(p > 0, 3, 2))

    def landed(j):
        return state.at[j, :, pl.ds(low, rows)]

    def first_copy(i):
        return pltpu.make_async_remote_copy(
            own.at[i], landed(i), z_send.at[i], z_recv.at[i],
            device_id=(below, q), device_id_type=MESH,
        )

    def pass_copy(j):
        return pltpu.make_async_remote_copy(
            landed(j), landed(block + j), z_send.at[block + j], z_recv.at[block + j],
            device_id=(below, q), device_id_type=MESH,
        )

    def side_copies(j):
        return (
            pltpu.make_async_remote_copy(
                state.at[j, :, pl.ds(low, halo)],
                state.at[j, :, pl.ds(high, halo)],
                x_send.at[0, j], x_recv.at[0, j],
                device_id=(p, left), device_id_type=MESH,
            ),
            pltpu.make_async_remote_copy(
                state.at[j, :, pl.ds(high - halo, halo)],
                state.at[j, :, pl.ds(PAD, halo)],
                x_send.at[1, j], x_recv.at[1, j],
                device_id=(p, right), device_id_type=MESH,
            ),
        )

    @pl.when(p > 0)
    def _():
        def send(i, carry):
            first_copy(i).start()
            return carry

        lax.fori_loop(0, block, send, 0)

    def arrive(j):
        @pl.when(p < peers - 1)
        def _():
            first_like = pltpu.make_async_remote_copy(
                landed(j), landed(j), z_send.at[j], z_recv.at[j],
                device_id=(below, q), device_id_type=MESH,
            )
            first_like.wait_recv()

        @pl.when((p > 0) & (j < stream - block))
        def _():
            pass_copy(j).start()

        for copy in side_copies(j):
            copy.start()

    gr = [[DT * grad[a, i] for i in range(3)] for a in range(4)]
    mid = [DT - 2.0 * (gr[a][0] + gr[a][1] + gr[a][2]) for a in range(4)]
    mid = [mid[a] + 1.0 for a in range(4)]
    cm = [0.25 * (comp[0, k] + comp[1, k] + comp[2, k] + comp[3, k]) for k in range(2)]
    beta = [[DT * (cm[k] - comp[a, k]) for k in range(2)] for a in range(3)]
    lm = 0.25 * (latent[0] + latent[1] + latent[2] + latent[3])
    gl = [DT * (lm - latent[a]) for a in range(3)]
    kd = [DT * diff[k] for k in range(2)]
    km = [1.0 - 6.0 * kd[k] for k in range(2)]
    rel = [[comp[a, k] - comp[3, k] for k in range(2)] for a in range(3)]
    flat3 = 2.0 * (gr[3][0] + gr[3][1] + gr[3][2]) + mid[3]

    def plane_step(s, j, source, target, edge):
        m = p * block + block + j
        turn = (s - 1) // STEPS
        top = planes - 1 + SHIFT * turn
        bottom = SHIFT * turn
        cen = j
        up = jnp.where(m == top, j, j + 1)
        down = jnp.where(m == bottom, j, j - 1)
        theta = (m.astype(jnp.float32) - 0.5 * planes) * (1.0 / planes)
        shift = [gl[a] * theta - 0.25 * flat3 + 0.25 for a in range(3)]

        def tile(at):
            here = pl.ds(at, HIGH)
            ctr, gs, xs, ys = [], [], [], []
            for f in range(FIELDS):
                c = source[cen, f, here]
                ctr.append(c)
                gs.append(source[up, f, here] + source[down, f, here])
                xs.append(source[cen, f, pl.ds(at - 1, HIGH)] + source[cen, f, pl.ds(at + 1, HIGH)])
                ys.append(pltpu.roll(c, 1, 1) + pltpu.roll(c, cols - 1, 1))
            w = [
                gr[a][0] * gs[a] + gr[a][1] * xs[a] + gr[a][2] * ys[a] + mid[a] * ctr[a]
                for a in range(3)
            ]
            w3 = (
                gr[3][0] * (gs[0] + gs[1] + gs[2])
                + gr[3][1] * (xs[0] + xs[1] + xs[2])
                + gr[3][2] * (ys[0] + ys[1] + ys[2])
                + mid[3] * (ctr[0] + ctr[1] + ctr[2])
            )
            mean = 0.25 * ((w[0] + w[1]) + (w[2] - w3))
            trial = [
                w[a] - mean + beta[a][0] * ctr[3] + beta[a][1] * ctr[4] + shift[a] for a in range(3)
            ]
            trial.append(1.0 - (trial[0] + trial[1] + trial[2]))
            clipped = [jnp.minimum(jnp.maximum(v, 0.0), 1.0) for v in trial]
            total = (clipped[0] + clipped[1]) + (clipped[2] + clipped[3])
            inv = pl.reciprocal(total, approx=True)
            inv = inv * (2.0 - total * inv)
            fresh = [clipped[a] * inv for a in range(3)]
            change = [fresh[a] - ctr[a] for a in range(3)]
            for k in range(2):
                around = (gs[3 + k] + xs[3 + k]) + ys[3 + k]
                value = km[k] * ctr[3 + k] + kd[k] * around
                fresh.append(value - (
                    rel[0][k] * change[0] + rel[1][k] * change[1] + rel[2][k] * change[2]
                ))
            put(at, HIGH, fresh)

        def put(at, size, fresh):
            if target is None:
                i = j - TOTAL
                out = pl.ds(at - low, size)
                for a in range(3):
                    phases[a, i, out] = fresh[a]
                phases[3, i, out] = 1.0 - (fresh[0] + fresh[1] + fresh[2])
                for k in range(2):
                    potentials[k, i, out] = fresh[3 + k]
            else:
                for f in range(FIELDS):
                    target[j, f, pl.ds(at, size)] = fresh[f]

        @pl.when(m <= top)
        def _():
            for at in range(PAD + 8 * edge, PAD + 2 * halo + rows - 8 * edge, HIGH):
                tile(at)

        @pl.when(m > top)
        def _():
            size = 2 * halo + rows - 16 * edge
            put(PAD + 8 * edge, size, [source[cen, f, pl.ds(PAD + 8 * edge, size)] for f in range(FIELDS)])

    for j in range(AHEAD):
        arrive(j)

    def diagonal(d, carry):
        @pl.when(d + AHEAD < stream)
        def _():
            arrive(d + AHEAD)

        for copy in side_copies(d):
            copy.wait_recv()

        @pl.when(d >= 2)
        def _():
            plane_step(1, d - 1, state, odd, 0)

        def pair(edge):
            def run(h, c):
                @pl.when(4 * h <= d)
                def _():
                    plane_step(2 * h, d - 2 * h, odd, even, edge)

                @pl.when(4 * h + 2 <= d)
                def _():
                    plane_step(2 * h + 1, d - 2 * h - 1, even, odd, edge)

                return c

            return run

        lax.fori_loop(1, 4, pair(0), 0)
        lax.fori_loop(4, 8, pair(1), 0)

        @pl.when(d >= 2 * TOTAL)
        def _():
            plane_step(TOTAL, d - TOTAL, odd, None, 2)

        return carry

    lax.fori_loop(0, stream, diagonal, 0)

    def settle(j, carry):
        for copy in side_copies(j):
            copy.wait_send()
        return carry

    lax.fori_loop(0, stream, settle, 0)

    @pl.when(p > 0)
    def _():
        def sent_own(i, carry):
            first_copy(i).wait_send()
            return carry

        lax.fori_loop(0, block, sent_own, 0)

        def sent_on(j, carry):
            pass_copy(j).wait_send()
            return carry

        lax.fori_loop(0, stream - block, sent_on, 0)


def solution(mesh):
    peers, lats = mesh.shape["grow"], mesh.shape["lat"]

    def on_device(labels, rough, pot, grad, comp, latent, diff, table, melt_index):
        block, rows, cols = labels.shape
        stream = block + 2 * TOTAL
        vmem = pl.BlockSpec(memory_space=pltpu.VMEM)
        smem = pl.BlockSpec(memory_space=pltpu.SMEM)
        return pl.pallas_call(
            functools.partial(kernel, peers, lats),
            out_shape=(
                jax.ShapeDtypeStruct((4, block, rows, cols), jnp.float32),
                jax.ShapeDtypeStruct((2, block, rows, cols), jnp.float32),
            ),
            in_specs=[vmem] * 4 + [smem] * 5,
            out_specs=(vmem, vmem),
            scratch_shapes=[
                pltpu.VMEM((block, FIELDS, rows, cols), jnp.float32),
                pltpu.VMEM((stream, FIELDS, rows + 2 * TOTAL + 2 * PAD, cols), jnp.float32),
pltpu.VMEM((stream, FIELDS, rows + 2 * TOTAL + 2 * PAD, cols), jnp.float32),
pltpu.VMEM((stream, FIELDS, rows + 2 * TOTAL + 2 * PAD, cols), jnp.float32),

                pltpu.SemaphoreType.DMA((stream,)),
                pltpu.SemaphoreType.DMA((stream,)),
                pltpu.SemaphoreType.DMA((2, stream)),
                pltpu.SemaphoreType.DMA((2, stream)),
            ],
            compiler_params=pltpu.CompilerParams(
                collective_id=0, has_side_effects=True, vmem_limit_bytes=48 << 20
            ),
        )(labels, rough, pot, melt_index, grad, comp, latent, diff, table)

    placed = (
        P("grow", "lat", None),
        P(None, "grow", "lat", None),
        P(None, "grow", "lat", None),
        P(),
        P(),
        P(),
        P(),
        P(),
        P(None, None, "lat", None),
    )
    return jax.shard_map(
        on_device,
        mesh=mesh,
        in_specs=placed,
        out_specs=(P(None, "grow", "lat", None), P(None, "grow", "lat", None)),
        check_vma=False,
    )
```

```python
import functools

import jax
import jax.numpy as jnp
from jax import lax
from jax.experimental import pallas as pl
from jax.experimental.pallas import tpu as pltpu
from jax.sharding import PartitionSpec as P

MESH = pl.DeviceIdType.MESH
STEPS = 4
ROUNDS = 4
SHIFT = 8
DT = 0.04
TOTAL = STEPS * ROUNDS
FIELDS = 5
PAD = 8
LEAD = 3
LINE = 8
GROUP = 3
GROUPS = 5
HIGH = 16


def kernel(
    peers,
    lats,
    labels,
    rough,
    pot,
    melt_index,
    grad,
    comp,
    latent,
    diff,
    table,
    phases,
    potentials,
    odd,
    even,
    z_send,
    z_recv,
    x_send,
    x_recv,
    own_send,
    own_recv,
    detour,
    d_send,
    d_recv,
):
    block, rows, cols = labels.shape
    halo = TOTAL
    low = PAD + halo
    high = low + rows
    planes = peers * block
    p = lax.axis_index("grow")
    q = lax.axis_index("lat")
    below = jnp.maximum(p - 1, 0)
    above = jnp.minimum(p + 1, peers - 1)
    z = lax.rem(p, LINE)
    turns = (z == 0) & (p >= LINE)
    helps = (z == 0) & (p < peers - LINE)
    left = lax.rem(q + lats - 1, lats)
    right = lax.rem(q + 1, lats)

    barrier = pltpu.get_barrier_semaphore()
    for side in (left, right):
        pl.semaphore_signal(barrier, inc=1, device_id=(p, side), device_id_type=MESH)

    @pl.when(p < peers - 1)
    def _():
        pl.semaphore_signal(barrier, inc=1, device_id=(above, q), device_id_type=MESH)

    @pl.when(helps)
    def _():
        pl.semaphore_signal(
            barrier, inc=1, device_id=(jnp.minimum(p + LINE, peers - 1), q), device_id_type=MESH
        )

    @pl.when((z == LINE - 1) & (p < peers - 1))
    def _():
        pl.semaphore_signal(
            barrier, inc=1, device_id=(jnp.maximum(p - LINE + 1, 0), q), device_id_type=MESH
        )

    def begin(i, carry):
        label = labels[i]
        parts = [rough[a, i] for a in range(4)]
        scale = 1.0 / (3.0 + (parts[0] + parts[1] + parts[2] + parts[3]))
        for a in range(3):
            even[i, a, pl.ds(low, rows)] = (jnp.where(label == a, 3.0, 0.0) + parts[a]) * scale
        for k in range(2):
            even[i, 3 + k, pl.ds(low, rows)] = pot[k, i]
        return carry

    lax.fori_loop(0, block, begin, 0)
    pl.semaphore_wait(
        barrier,
        2 + (p > 0).astype(jnp.int32) + turns.astype(jnp.int32) + helps.astype(jnp.int32),
    )

    def down_copies(t, field):
        return [
            pltpu.make_async_remote_copy(
                field.at[2 * t + l, :, pl.ds(low, rows)],
                field.at[2 * t + block + l, :, pl.ds(low, rows)],
                z_send.at[t, l],
                z_recv.at[t, l],
                device_id=(below, q),
                device_id_type=MESH,
            )
            for l in range(LEAD)
        ]

    def turn_copies(k):
        return [
            pltpu.make_async_remote_copy(
                odd.at[4 * k + 2 + l, :, pl.ds(low, rows)],
                detour.at[k, l],
                z_send.at[2 * k + 1, l],
                d_recv.at[k, l],
                device_id=(jnp.maximum(p - LINE, 0), q),
                device_id_type=MESH,
            )
            for l in range(LEAD)
        ]

    def help_copies(k):
        return [
            pltpu.make_async_remote_copy(
                detour.at[k, l],
                odd.at[4 * k + 2 + block + l, :, pl.ds(low, rows)],
                d_send.at[k, l],
                z_recv.at[2 * k + 1, l],
                device_id=(jnp.minimum(p + LINE - 1, peers - 1), q),
                device_id_type=MESH,
            )
            for l in range(LEAD)
        ]

    def halo_copies(field, at, count, width, send, recv):
        return (
            pltpu.make_async_remote_copy(
                field.at[pl.ds(at, count), :, pl.ds(low, width)],
                field.at[pl.ds(at, count), :, pl.ds(high, width)],
                send.at[0], recv.at[0],
                device_id=(p, left), device_id_type=MESH,
            ),
            pltpu.make_async_remote_copy(
                field.at[pl.ds(at, count), :, pl.ds(high - width, width)],
                field.at[pl.ds(at, count), :, pl.ds(low - width, width)],
                send.at[1], recv.at[1],
                device_id=(p, right), device_id_type=MESH,
            ),
        )

    def own_copies(c):
        return halo_copies(even, 4 * c, 4, halo, own_send.at[c], own_recv.at[c])

    def side_copies(t, field, width):
        return halo_copies(field, 2 * t + block, LEAD, width, x_send.at[t], x_recv.at[t])

    def by_level(t, use):
        for parity, field in ((0, even), (1, odd)):
            for first, width in ((0, 16), (8, 8)):
                @pl.when((lax.rem(t, 2) == parity) & (t >= first) & (t < first + 8))
                def _():
                    use(field, width)

    for c in range(2):
        for copy in own_copies(c):
            copy.start()

    @pl.when(p > 0)
    def _():
        for copy in down_copies(0, even):
            copy.start()

    for c in range(2, 4):
        for copy in own_copies(c):
            copy.start()

    def melt(t, field):
        for l in range(LEAD):
            j = jnp.minimum(2 * t + l, ROUNDS * SHIFT - 1)
            chosen = melt_index[j // SHIFT, lax.rem(j, SHIFT)]
            zero = jnp.zeros((rows, cols), jnp.float32)
            for a in range(3):
                field[2 * t + block + l, a, pl.ds(low, rows)] = zero
            for k in range(2):
                value = zero + table[0, k]
                for e in range(1, table.shape[0]):
                    value = jnp.where(chosen == e, table[e, k], value)
                field[2 * t + block + l, 3 + k, pl.ds(low, rows)] = value

    def arrive(t):
        @pl.when(p < peers - 1)
        def _():
            for copy in down_copies(t, even):
                copy.wait_recv()

        @pl.when((p == peers - 1) & (lax.rem(t, 2) == 0))
        def _():
            melt(t, even)

        @pl.when((p == peers - 1) & (lax.rem(t, 2) == 1))
        def _():
            melt(t, odd)

        def go(field, width):
            for copy in side_copies(t, field, width):
                copy.start()

        by_level(t, go)

    def sides_done(t):
        def go(field, width):
            for copy in side_copies(t, field, width):
                copy.wait()

        by_level(t, go)

    gr = [[DT * grad[a, i] for i in range(3)] for a in range(4)]
    mid = [DT - 2.0 * (gr[a][0] + gr[a][1] + gr[a][2]) for a in range(4)]
    mid = [mid[a] + 1.0 for a in range(4)]
    cm = [0.25 * (comp[0, k] + comp[1, k] + comp[2, k] + comp[3, k]) for k in range(2)]
    beta = [[DT * (cm[k] - comp[a, k]) for k in range(2)] for a in range(3)]
    lm = 0.25 * (latent[0] + latent[1] + latent[2] + latent[3])
    gl = [DT * (lm - latent[a]) for a in range(3)]
    kd = [DT * diff[k] for k in range(2)]
    km = [1.0 - 6.0 * kd[k] for k in range(2)]
    rel = [[comp[a, k] - comp[3, k] for k in range(2)] for a in range(3)]
    flat3 = 2.0 * (gr[3][0] + gr[3][1] + gr[3][2]) + mid[3]

    def plane_step(s, j, source, target, edge):
        m = p * block + j
        turn = (s - 1) // STEPS
        top = planes - 1 + SHIFT * turn
        bottom = SHIFT * turn
        cen = j
        up = jnp.where(m == top, j, j + 1)
        down = jnp.where(m == bottom, j, j - 1)
        theta = (m.astype(jnp.float32) - 0.5 * planes) * (1.0 / planes)
        shift = [gl[a] * theta - 0.25 * flat3 + 0.25 for a in range(3)]

        def tile(at):
            here = pl.ds(at, HIGH)
            ctr, gs, xs, ys = [], [], [], []
            for f in range(FIELDS):
                c = source[cen, f, here]
                ctr.append(c)
                gs.append(source[up, f, here] + source[down, f, here])
                xs.append(source[cen, f, pl.ds(at - 1, HIGH)] + source[cen, f, pl.ds(at + 1, HIGH)])
                ys.append(pltpu.roll(c, 1, 1) + pltpu.roll(c, cols - 1, 1))
            w = [
                gr[a][0] * gs[a] + gr[a][1] * xs[a] + gr[a][2] * ys[a] + mid[a] * ctr[a]
                for a in range(3)
            ]
            w3 = (
                gr[3][0] * (gs[0] + gs[1] + gs[2])
                + gr[3][1] * (xs[0] + xs[1] + xs[2])
                + gr[3][2] * (ys[0] + ys[1] + ys[2])
                + mid[3] * (ctr[0] + ctr[1] + ctr[2])
            )
            mean = 0.25 * ((w[0] + w[1]) + (w[2] - w3))
            trial = [
                w[a] - mean + beta[a][0] * ctr[3] + beta[a][1] * ctr[4] + shift[a] for a in range(3)
            ]
            trial.append(1.0 - (trial[0] + trial[1] + trial[2]))
            clipped = [jnp.minimum(jnp.maximum(v, 0.0), 1.0) for v in trial]
            total = (clipped[0] + clipped[1]) + (clipped[2] + clipped[3])
            inv = pl.reciprocal(total, approx=True)
            inv = inv * (2.0 - total * inv)
            fresh = [clipped[a] * inv for a in range(3)]
            change = [fresh[a] - ctr[a] for a in range(3)]
            for k in range(2):
                around = (gs[3 + k] + xs[3 + k]) + ys[3 + k]
                value = km[k] * ctr[3 + k] + kd[k] * around
                fresh.append(value - (
                    rel[0][k] * change[0] + rel[1][k] * change[1] + rel[2][k] * change[2]
                ))
            put(at, HIGH, fresh)

        def put(at, size, fresh):
            if target is None:
                i = j - 2 * TOTAL
                out = pl.ds(at - low, size)
                for a in range(3):
                    phases[a, i, out] = fresh[a]
                phases[3, i, out] = 1.0 - (fresh[0] + fresh[1] + fresh[2])
                for k in range(2):
                    potentials[k, i, out] = fresh[3 + k]
            else:
                for f in range(FIELDS):
                    target[j, f, pl.ds(at, size)] = fresh[f]

        @pl.when(m <= top)
        def _():
            for at in range(PAD + 8 * edge, PAD + 2 * halo + rows - 8 * edge, HIGH):
                tile(at)

        @pl.when(m > top)
        def _():
            size = 2 * halo + rows - 16 * edge
            put(PAD + 8 * edge, size, [source[cen, f, pl.ds(PAD + 8 * edge, size)] for f in range(FIELDS)])

    def group(g, level):
        first = 2 * level + GROUP * g
        last = first + GROUP + jnp.where(g == GROUPS - 1, block - GROUP * GROUPS, 0)

        def run(source, target, edge):
            def one(j, c):
                plane_step(level, j, source, target, edge)
                return c

            lax.fori_loop(first, last, one, 0)

        for parity, source, target in ((1, even, odd), (0, odd, even)):
            for edge in range(2):
                @pl.when((lax.rem(level, 2) == parity) & (level // 8 == edge))
                def _():
                    run(source, target, edge)

        @pl.when(level == TOTAL)
        def _():
            run(odd, None, 2)

    def iteration(n, carry):
        @pl.when((n >= GROUPS - 1) & (n - GROUPS + 1 < TOTAL))
        def _():
            arrive(n - GROUPS + 1)

        def descend(k, c):
            g = GROUPS - 1 - k
            level = n - g

            @pl.when((g == GROUPS - 1) & (level >= 1))
            def _():
                sides_done(level - 1)

            @pl.when(level == 1)
            def _():
                for c in range(4):
                    @pl.when(g == max(c - 1, 0))
                    def _():
                        for copy in own_copies(c):
                            copy.wait()

            @pl.when((level >= 1) & (level <= TOTAL))
            def _():
                group(g, level)

            return c

        lax.fori_loop(0, GROUPS, descend, 0)

        @pl.when(helps & (n >= 3) & (n - 2 < TOTAL) & (lax.rem(n, 2) == 1))
        def _():
            for copy in turn_copies((n - 2) // 2):
                copy.wait_recv()
            for copy in help_copies((n - 2) // 2):
                copy.start()

        @pl.when((p > 0) & (n < TOTAL) & (lax.rem(n, 2) == 0))
        def _():
            for copy in down_copies(n, even):
                copy.start()

        @pl.when((p > 0) & (z > 0) & (n < TOTAL) & (lax.rem(n, 2) == 1))
        def _():
            for copy in down_copies(n, odd):
                copy.start()

        @pl.when(turns & (n < TOTAL) & (lax.rem(n, 2) == 1))
        def _():
            for copy in turn_copies(n // 2):
                copy.start()

        return carry

    lax.fori_loop(1, TOTAL + GROUPS, iteration, 0)

    @pl.when(p > 0)
    def _():
        def sent(t, carry):
            for copy in down_copies(t, even):
                copy.wait_send()
            return carry

        lax.fori_loop(0, TOTAL, sent, 0)

    @pl.when(helps)
    def _():
        def helped(k, carry):
            for copy in help_copies(k):
                copy.wait_send()
            return carry

        lax.fori_loop(0, TOTAL // 2, helped, 0)


def solution(mesh):
    peers, lats = mesh.shape["grow"], mesh.shape["lat"]

    def on_device(labels, rough, pot, grad, comp, latent, diff, table, melt_index):
        block, rows, cols = labels.shape
        span = block + 2 * TOTAL + LEAD
        field = pltpu.VMEM((span, FIELDS, rows + 2 * TOTAL + 2 * PAD, cols), jnp.float32)
        vmem = pl.BlockSpec(memory_space=pltpu.VMEM)
        smem = pl.BlockSpec(memory_space=pltpu.SMEM)
        return pl.pallas_call(
            functools.partial(kernel, peers, lats),
            out_shape=(
                jax.ShapeDtypeStruct((4, block, rows, cols), jnp.float32),
                jax.ShapeDtypeStruct((2, block, rows, cols), jnp.float32),
            ),
            in_specs=[vmem] * 4 + [smem] * 5,
            out_specs=(vmem, vmem),
            scratch_shapes=[field, field] + [
                pltpu.SemaphoreType.DMA((TOTAL, LEAD)),
                pltpu.SemaphoreType.DMA((TOTAL, LEAD)),
                pltpu.SemaphoreType.DMA((TOTAL, 2)),
                pltpu.SemaphoreType.DMA((TOTAL, 2)),
                pltpu.SemaphoreType.DMA((4, 2)),
                pltpu.SemaphoreType.DMA((4, 2)),
                pltpu.VMEM((TOTAL // 2, LEAD, FIELDS, rows, cols), jnp.float32),
                pltpu.SemaphoreType.DMA((TOTAL // 2, LEAD)),
                pltpu.SemaphoreType.DMA((TOTAL // 2, LEAD)),
            ],
            compiler_params=pltpu.CompilerParams(
                collective_id=0, has_side_effects=True, vmem_limit_bytes=48 << 20
            ),
        )(labels, rough, pot, melt_index, grad, comp, latent, diff, table)

    placed = (
        P("grow", "lat", None),
        P(None, "grow", "lat", None),
        P(None, "grow", "lat", None),
        P(),
        P(),
        P(),
        P(),
        P(),
        P(None, None, "lat", None),
    )
    return jax.shard_map(
        on_device,
        mesh=mesh,
        in_specs=placed,
        out_specs=(P(None, "grow", "lat", None), P(None, "grow", "lat", None)),
        check_vma=False,
    )
```

```python
import functools

import jax
import jax.numpy as jnp
from jax import lax
from jax.experimental import pallas as pl
from jax.experimental.pallas import tpu as pltpu
from jax.sharding import PartitionSpec as P

MESH = pl.DeviceIdType.MESH
STEPS = 4
ROUNDS = 4
SHIFT = 8
DT = 0.04
TOTAL = STEPS * ROUNDS
FIELDS = 5
PAD = 8
LEAD = 3
LINE = 8
HALO = 8
HELP_AT = 2
GROUP = 3
GROUPS = 5
HIGH = 16


def kernel(
    peers,
    lats,
    labels_in,
    rough_in,
    pot_in,
    melt_in,
    grad,
    comp,
    latent,
    diff,
    table,
    phases,
    potentials,
    odd,
    even,
    z_send,
    z_recv,
    x_send,
    x_recv,
    own_send,
    own_recv,
    detour,
    d_send,
    d_recv,
    labels,
    rough,
    pot,
    melt_index,
    load,
):
    block, rows, cols = labels.shape
    halo = HALO
    low = PAD + halo
    high = low + rows
    planes = peers * block
    p = lax.axis_index("grow")
    q = lax.axis_index("lat")
    below = jnp.maximum(p - 1, 0)
    above = jnp.minimum(p + 1, peers - 1)
    z = lax.rem(p, LINE)
    turns = (z == 0) & (p >= LINE)
    helps = (z == 0) & (p < peers - LINE)
    left = lax.rem(q + lats - 1, lats)
    right = lax.rem(q + 1, lats)

    def loads(c):
        some = pl.ds(4 * c, 4)
        return (
            pltpu.make_async_copy(labels_in.at[some], labels.at[some], load.at[3 * c]),
            pltpu.make_async_copy(rough_in.at[:, some], rough.at[:, some], load.at[3 * c + 1]),
            pltpu.make_async_copy(pot_in.at[:, some], pot.at[:, some], load.at[3 * c + 2]),
        )

    melt_load = pltpu.make_async_copy(melt_in, melt_index, load.at[12])
    for c in range(4):
        for copy in loads(c):
            copy.start()

    barrier = pltpu.get_barrier_semaphore()
    for side in (left, right):
        pl.semaphore_signal(barrier, inc=1, device_id=(p, side), device_id_type=MESH)

    @pl.when(p < peers - 1)
    def _():
        pl.semaphore_signal(barrier, inc=1, device_id=(above, q), device_id_type=MESH)

    @pl.when(helps)
    def _():
        pl.semaphore_signal(
            barrier, inc=1, device_id=(jnp.minimum(p + LINE, peers - 1), q), device_id_type=MESH
        )

    @pl.when((z == LINE - 1) & (p < peers - 1))
    def _():
        pl.semaphore_signal(
            barrier, inc=1, device_id=(jnp.maximum(p - LINE + 1, 0), q), device_id_type=MESH
        )

    def begin(i, carry):
        label = labels[i]
        parts = [rough[a, i] for a in range(4)]
        scale = 1.0 / (3.0 + (parts[0] + parts[1] + parts[2] + parts[3]))
        for a in range(3):
            even[i, a, pl.ds(low, rows)] = (jnp.where(label == a, 3.0, 0.0) + parts[a]) * scale
        for k in range(2):
            even[i, 3 + k, pl.ds(low, rows)] = pot[k, i]
        return carry

    def start_part(c):
        for copy in loads(c):
            copy.wait()
        lax.fori_loop(4 * c, 4 * c + 4, begin, 0)

    start_part(0)
    pl.semaphore_wait(
        barrier,
        2 + (p > 0).astype(jnp.int32) + turns.astype(jnp.int32) + helps.astype(jnp.int32),
    )

    def lands(t, l, field):
        return field.at[2 * t + block + l, :, pl.ds(low, rows)]

    def down_copy(t, l, field):
        return pltpu.make_async_remote_copy(
            field.at[2 * t + l, :, pl.ds(low, rows)],
            lands(t, l, field),
            z_send.at[t, l],
            z_recv.at[t, l],
            device_id=(below, q),
            device_id_type=MESH,
        )

    def turn_copy(t, l, field):
        return pltpu.make_async_remote_copy(
            field.at[2 * t + l, :, pl.ds(low, rows)],
            detour.at[t, l],
            z_send.at[t, l],
            d_recv.at[t, l],
            device_id=(jnp.maximum(p - LINE, 0), q),
            device_id_type=MESH,
        )

    def help_copy(t, l, field):
        return pltpu.make_async_remote_copy(
            detour.at[t, l],
            lands(t, l, field),
            d_send.at[t, l],
            z_recv.at[t, l],
            device_id=(jnp.minimum(p + LINE - 1, peers - 1), q),
            device_id_type=MESH,
        )

    def send_down(t, parity, field):
        @pl.when(turns)
        def _():
            for l in range(LEAD):
                (turn_copy if l <= parity else down_copy)(t, l, field).start()

        @pl.when((p > 0) & (z > 0))
        def _():
            for l in range(LEAD):
                down_copy(t, l, field).start()

    def help_down(t, parity, field):
        for l in range(parity + 1):
            turn_copy(t, l, field).wait_recv()
            help_copy(t, l, field).start()

    def halo_copies(field, at, count, send, recv):
        return (
            pltpu.make_async_remote_copy(
                field.at[pl.ds(at, count), :, pl.ds(low, halo)],
                field.at[pl.ds(at, count), :, pl.ds(high, halo)],
                send.at[0], recv.at[0],
                device_id=(p, left), device_id_type=MESH,
            ),
            pltpu.make_async_remote_copy(
                field.at[pl.ds(at, count), :, pl.ds(high - halo, halo)],
                field.at[pl.ds(at, count), :, pl.ds(low - halo, halo)],
                send.at[1], recv.at[1],
                device_id=(p, right), device_id_type=MESH,
            ),
        )

    def own_copies(c):
        return halo_copies(even, 4 * c, 4, own_send.at[c], own_recv.at[c])

    def side_copies(t, field):
        return halo_copies(field, 2 * t + block, LEAD, x_send.at[t], x_recv.at[t])

    send_down(0, 0, even)

    for c in range(4):
        if c > 0:
            start_part(c)
        for copy in own_copies(c):
            copy.start()

    @pl.when(p == peers - 1)
    def _():
        melt_load.start()
        melt_load.wait()

    def melt(t, field):
        for l in range(LEAD):
            j = jnp.minimum(2 * t + l, ROUNDS * SHIFT - 1)
            chosen = melt_index[j // SHIFT, lax.rem(j, SHIFT)]
            zero = jnp.zeros((rows, cols), jnp.float32)
            for a in range(3):
                field[2 * t + block + l, a, pl.ds(low, rows)] = zero
            for k in range(2):
                value = zero + table[k, 0]
                for e in range(1, table.shape[1]):
                    value = jnp.where(chosen == e, table[k, e], value)
                field[2 * t + block + l, 3 + k, pl.ds(low, rows)] = value

    def arrive(t):
        @pl.when(p < peers - 1)
        def _():
            for l in range(LEAD):
                down_copy(t, l, even).wait_recv()

        for parity, field in ((0, even), (1, odd)):
            @pl.when((p == peers - 1) & (lax.rem(t, 2) == parity))
            def _():
                melt(t, field)

            @pl.when(lax.rem(t, 2) == parity)
            def _():
                for copy in side_copies(t, field):
                    copy.start()

    def sides_done(t):
        for parity, field in ((0, even), (1, odd)):
            @pl.when(lax.rem(t, 2) == parity)
            def _():
                for copy in side_copies(t, field):
                    copy.wait()

    gr = [[DT * grad[a, i] for i in range(3)] for a in range(4)]
    mid = [DT - 2.0 * (gr[a][0] + gr[a][1] + gr[a][2]) for a in range(4)]
    mid = [mid[a] + 1.0 for a in range(4)]
    cm = [0.25 * (comp[k, 0] + comp[k, 1] + comp[k, 2] + comp[k, 3]) for k in range(2)]
    beta = [[DT * (cm[k] - comp[k, a]) for k in range(2)] for a in range(3)]
    lm = 0.25 * (latent[0] + latent[1] + latent[2] + latent[3])
    gl = [DT * (lm - latent[a]) for a in range(3)]
    kd = [DT * diff[k] for k in range(2)]
    km = [1.0 - 6.0 * kd[k] for k in range(2)]
    rel = [[comp[k, a] - comp[k, 3] for k in range(2)] for a in range(3)]
    flat3 = 2.0 * (gr[3][0] + gr[3][1] + gr[3][2]) + mid[3]

    def plane_step(s, j, source, target, edge):
        m = p * block + j
        turn = (s - 1) // STEPS
        top = planes - 1 + SHIFT * turn
        bottom = SHIFT * turn
        cen = j
        up = jnp.where(m == top, j, j + 1)
        down = jnp.where(m == bottom, j, j - 1)
        theta = (m.astype(jnp.float32) - 0.5 * planes) * (1.0 / planes)
        shift = [gl[a] * theta - 0.25 * flat3 + 0.25 for a in range(3)]

        def tile(at):
            here = pl.ds(at, HIGH)
            ctr, gs, xs, ys = [], [], [], []
            for f in range(FIELDS):
                c = source[cen, f, here]
                ctr.append(c)
                gs.append(source[up, f, here] + source[down, f, here])
                xs.append(source[cen, f, pl.ds(at - 1, HIGH)] + source[cen, f, pl.ds(at + 1, HIGH)])
                ys.append(pltpu.roll(c, 1, 1) + pltpu.roll(c, cols - 1, 1))
            w = [
                gr[a][0] * gs[a] + gr[a][1] * xs[a] + gr[a][2] * ys[a] + mid[a] * ctr[a]
                for a in range(3)
            ]
            w3 = (
                gr[3][0] * (gs[0] + gs[1] + gs[2])
                + gr[3][1] * (xs[0] + xs[1] + xs[2])
                + gr[3][2] * (ys[0] + ys[1] + ys[2])
                + mid[3] * (ctr[0] + ctr[1] + ctr[2])
            )
            mean = 0.25 * ((w[0] + w[1]) + (w[2] - w3))
            trial = [
                w[a] - mean + beta[a][0] * ctr[3] + beta[a][1] * ctr[4] + shift[a] for a in range(3)
            ]
            trial.append(1.0 - (trial[0] + trial[1] + trial[2]))
            clipped = [jnp.minimum(jnp.maximum(v, 0.0), 1.0) for v in trial]
            total = (clipped[0] + clipped[1]) + (clipped[2] + clipped[3])
            inv = pl.reciprocal(total, approx=True)
            inv = inv * (2.0 - total * inv)
            fresh = [clipped[a] * inv for a in range(3)]
            change = [fresh[a] - ctr[a] for a in range(3)]
            for k in range(2):
                around = (gs[3 + k] + xs[3 + k]) + ys[3 + k]
                value = km[k] * ctr[3 + k] + kd[k] * around
                fresh.append(value - (
                    rel[0][k] * change[0] + rel[1][k] * change[1] + rel[2][k] * change[2]
                ))
            put(at, HIGH, fresh)

        def put(at, size, fresh):
            if target is None:
                i = j - 2 * TOTAL
                out = pl.ds(at - low, size)
                for a in range(3):
                    phases[a, i, out] = fresh[a]
                phases[3, i, out] = 1.0 - (fresh[0] + fresh[1] + fresh[2])
                for k in range(2):
                    potentials[k, i, out] = fresh[3 + k]
            else:
                for f in range(FIELDS):
                    target[j, f, pl.ds(at, size)] = fresh[f]

        @pl.when(m <= top)
        def _():
            for at in range(PAD + 8 * edge, PAD + 2 * halo + rows - 8 * edge, HIGH):
                tile(at)

        @pl.when(m > top)
        def _():
            size = 2 * halo + rows - 16 * edge
            put(PAD + 8 * edge, size, [source[cen, f, pl.ds(PAD + 8 * edge, size)] for f in range(FIELDS)])

    def group(g, level):
        first = 2 * level + GROUP * g
        last = first + GROUP + jnp.where(g == GROUPS - 1, block - GROUP * GROUPS, 0)

        lowest = first + jnp.where(g == 0, 2, 0)

        def run(source, target, edge, begin, end):
            def one(j, c):
                plane_step(level, j, source, target, edge)
                return c

            lax.fori_loop(begin, end, one, 0)

        for parity, source, target in ((1, even, odd), (0, odd, even)):
            @pl.when((lax.rem(level, 2) == parity) & (level < TOTAL))
            def _():
                run(source, target, 1, first, lowest)
                run(source, target, 0, lowest, last)

        @pl.when(level == TOTAL)
        def _():
            run(odd, None, 1, first, last)

    def iteration(n, carry):
        @pl.when((n >= GROUPS - 1) & (n - GROUPS + 1 < TOTAL))
        def _():
            arrive(n - GROUPS + 1)

        def descend(k, c):
            g = GROUPS - 1 - k
            level = n - g

            @pl.when((g == GROUPS - 1) & (level >= 1))
            def _():
                sides_done(level - 1)

            @pl.when(level == 1)
            def _():
                for c in range(4):
                    @pl.when(g == max(c - 1, 0))
                    def _():
                        for copy in own_copies(c):
                            copy.wait()

            @pl.when((level >= 1) & (level <= TOTAL))
            def _():
                group(g, level)

            for parity, field in ((0, even), (1, odd)):
                @pl.when(
                    helps & (k == HELP_AT) & (n >= 2) & (n - 2 < TOTAL) & (lax.rem(n, 2) == parity)
                )
                def _():
                    help_down(n - 2, parity, field)

            return c

        lax.fori_loop(0, GROUPS, descend, 0)

        for parity, field in ((0, even), (1, odd)):
            @pl.when((n < TOTAL) & (lax.rem(n, 2) == parity))
            def _():
                send_down(n, parity, field)

        return carry

    lax.fori_loop(1, TOTAL + GROUPS, iteration, 0)

    @pl.when(p > 0)
    def _():
        def sent(t, carry):
            for l in range(LEAD):
                down_copy(t, l, even).wait_send()
            return carry

        lax.fori_loop(0, TOTAL, sent, 0)

    @pl.when(helps)
    def _():
        def helped(h, carry):
            for parity, field in ((0, even), (1, odd)):
                for l in range(parity + 1):
                    help_copy(2 * h + parity, l, field).wait_send()
            return carry

        lax.fori_loop(0, TOTAL // 2, helped, 0)


def solution(mesh):
    peers, lats = mesh.shape["grow"], mesh.shape["lat"]

    def on_device(labels, rough, pot, grad, comp, latent, diff, table, melt_index):
        block, rows, cols = labels.shape
        span = block + 2 * TOTAL + LEAD
        field = pltpu.VMEM((span, FIELDS, rows + 2 * HALO + 2 * PAD, cols), jnp.float32)
        vmem = pl.BlockSpec(memory_space=pltpu.VMEM)
        hbm = pl.BlockSpec(memory_space=pltpu.HBM)
        smem = pl.BlockSpec(memory_space=pltpu.SMEM)
        return pl.pallas_call(
            functools.partial(kernel, peers, lats),
            out_shape=(
                jax.ShapeDtypeStruct((4, block, rows, cols), jnp.float32),
                jax.ShapeDtypeStruct((2, block, rows, cols), jnp.float32),
            ),
            in_specs=[hbm] * 4 + [smem] * 5,
            out_specs=(vmem, vmem),
            scratch_shapes=[field, field] + [
                pltpu.SemaphoreType.DMA((TOTAL, LEAD)),
                pltpu.SemaphoreType.DMA((TOTAL, LEAD)),
                pltpu.SemaphoreType.DMA((TOTAL, 2)),
                pltpu.SemaphoreType.DMA((TOTAL, 2)),
                pltpu.SemaphoreType.DMA((4, 2)),
                pltpu.SemaphoreType.DMA((4, 2)),
                pltpu.VMEM((TOTAL, 2, FIELDS, rows, cols), jnp.float32),
                pltpu.SemaphoreType.DMA((TOTAL, 2)),
                pltpu.SemaphoreType.DMA((TOTAL, 2)),
                pltpu.VMEM((block, rows, cols), jnp.int32),
                pltpu.VMEM((4, block, rows, cols), jnp.float32),
                pltpu.VMEM((2, block, rows, cols), jnp.float32),
                pltpu.VMEM((ROUNDS, SHIFT, rows, cols), jnp.int32),
                pltpu.SemaphoreType.DMA((13,)),
            ],
            compiler_params=pltpu.CompilerParams(
                collective_id=0, has_side_effects=True, vmem_limit_bytes=60 << 20
            ),
        )(labels, rough, pot, melt_index, grad, comp.T, latent, diff, table.T)

    placed = (
        P("grow", "lat", None),
        P(None, "grow", "lat", None),
        P(None, "grow", "lat", None),
        P(),
        P(),
        P(),
        P(),
        P(),
        P(None, None, "lat", None),
    )
    return jax.shard_map(
        on_device,
        mesh=mesh,
        in_specs=placed,
        out_specs=(P(None, "grow", "lat", None), P(None, "grow", "lat", None)),
        check_vma=False,
    )
```

```python
import functools

import jax
import jax.numpy as jnp
from jax import lax
from jax.experimental import pallas as pl
from jax.experimental.pallas import tpu as pltpu
from jax.sharding import PartitionSpec as P

MESH = pl.DeviceIdType.MESH
STEPS = 4
ROUNDS = 4
SHIFT = 8
DT = 0.04
TOTAL = STEPS * ROUNDS
FIELDS = 5
PAD = 8
LEAD = 3
LINE = 8
HALO = 8
HELP_AT = 3
GROUP = 3
GROUPS = 5
HIGH = 16


def kernel(
    peers,
    lats,
    labels_in,
    rough_in,
    pot_in,
    melt_in,
    grad,
    comp,
    latent,
    diff,
    table,
    phases_out,
    potentials_out,
    odd,
    even,
    z_send,
    z_recv,
    x_send,
    x_recv,
    own_send,
    own_recv,
    detour,
    d_send,
    d_recv,
    labels,
    rough,
    pot,
    melt_index,
    load,
    phases,
    potentials,
    store,
):
    block, rows, cols = labels.shape
    halo = HALO
    low = PAD + halo
    high = low + rows
    planes = peers * block
    p = lax.axis_index("grow")
    q = lax.axis_index("lat")
    below = jnp.maximum(p - 1, 0)
    above = jnp.minimum(p + 1, peers - 1)
    z = lax.rem(p, LINE)
    turns = (z == 0) & (p >= LINE)
    helps = (z == 0) & (p < peers - LINE)
    left = lax.rem(q + lats - 1, lats)
    right = lax.rem(q + 1, lats)

    def loads(c):
        some = pl.ds(4 * c, 4)
        return (
            pltpu.make_async_copy(labels_in.at[some], labels.at[some], load.at[3 * c]),
            pltpu.make_async_copy(rough_in.at[:, some], rough.at[:, some], load.at[3 * c + 1]),
            pltpu.make_async_copy(pot_in.at[:, some], pot.at[:, some], load.at[3 * c + 2]),
        )

    melt_load = pltpu.make_async_copy(melt_in, melt_index, load.at[12])
    barrier = pltpu.get_barrier_semaphore()
    for side in (left, right):
        pl.semaphore_signal(barrier, inc=1, device_id=(p, side), device_id_type=MESH)

    @pl.when(p < peers - 1)
    def _():
        pl.semaphore_signal(barrier, inc=1, device_id=(above, q), device_id_type=MESH)

    @pl.when(helps)
    def _():
        pl.semaphore_signal(
            barrier, inc=1, device_id=(jnp.minimum(p + LINE, peers - 1), q), device_id_type=MESH
        )

    @pl.when((z == LINE - 1) & (p < peers - 1))
    def _():
        pl.semaphore_signal(
            barrier, inc=1, device_id=(jnp.maximum(p - LINE + 1, 0), q), device_id_type=MESH
        )

    for c in range(4):
        for copy in loads(c):
            copy.start()

    def stores(i):
        return (
            pltpu.make_async_copy(phases.at[:, i], phases_out.at[:, i], store.at[i, 0]),
            pltpu.make_async_copy(potentials.at[:, i], potentials_out.at[:, i], store.at[i, 1]),
        )

    def begin(i, carry):
        label = labels[i]
        parts = [rough[a, i] for a in range(4)]
        scale = 1.0 / (3.0 + (parts[0] + parts[1] + parts[2] + parts[3]))
        for a in range(3):
            even[i, a, pl.ds(low, rows)] = (jnp.where(label == a, 3.0, 0.0) + parts[a]) * scale
        for k in range(2):
            even[i, 3 + k, pl.ds(low, rows)] = pot[k, i]
        return carry

    def start_part(c):
        for copy in loads(c):
            copy.wait()
        lax.fori_loop(4 * c, 4 * c + 4, begin, 0)

    start_part(0)
    pl.semaphore_wait(
        barrier,
        2 + (p > 0).astype(jnp.int32) + turns.astype(jnp.int32) + helps.astype(jnp.int32),
    )

    def lands(t, l, field):
        return field.at[2 * t + block + l, :, pl.ds(low, rows)]

    def down_copy(t, l, field):
        return pltpu.make_async_remote_copy(
            field.at[2 * t + l, :, pl.ds(low, rows)],
            lands(t, l, field),
            z_send.at[t, l],
            z_recv.at[t, l],
            device_id=(below, q),
            device_id_type=MESH,
        )

    def turn_copy(t, l, field):
        return pltpu.make_async_remote_copy(
            field.at[2 * t + l, :, pl.ds(low, rows)],
            detour.at[t, l],
            z_send.at[t, l],
            d_recv.at[t, l],
            device_id=(jnp.maximum(p - LINE, 0), q),
            device_id_type=MESH,
        )

    def help_copy(t, l, field):
        return pltpu.make_async_remote_copy(
            detour.at[t, l],
            lands(t, l, field),
            d_send.at[t, l],
            z_recv.at[t, l],
            device_id=(jnp.minimum(p + LINE - 1, peers - 1), q),
            device_id_type=MESH,
        )

    def send_down(t, parity, field):
        @pl.when(turns)
        def _():
            for l in range(LEAD):
                (turn_copy if l <= parity else down_copy)(t, l, field).start()

        @pl.when((p > 0) & (z > 0))
        def _():
            for l in range(LEAD):
                down_copy(t, l, field).start()

    def help_down(t, parity, field):
        for l in range(parity + 1):
            turn_copy(t, l, field).wait_recv()
            help_copy(t, l, field).start()

    def halo_copies(field, at, count, send, recv):
        return (
            pltpu.make_async_remote_copy(
                field.at[pl.ds(at, count), :, pl.ds(low, halo)],
                field.at[pl.ds(at, count), :, pl.ds(high, halo)],
                send.at[0], recv.at[0],
                device_id=(p, left), device_id_type=MESH,
            ),
            pltpu.make_async_remote_copy(
                field.at[pl.ds(at, count), :, pl.ds(high - halo, halo)],
                field.at[pl.ds(at, count), :, pl.ds(low - halo, halo)],
                send.at[1], recv.at[1],
                device_id=(p, right), device_id_type=MESH,
            ),
        )

    def own_copies(c):
        return halo_copies(even, 4 * c, 4, own_send.at[c], own_recv.at[c])

    def side_copies(t, field):
        return halo_copies(field, 2 * t + block, LEAD, x_send.at[t], x_recv.at[t])

    send_down(0, 0, even)

    for c in range(4):
        if c > 0:
            start_part(c)
        for copy in own_copies(c):
            copy.start()

    @pl.when(p == peers - 1)
    def _():
        melt_load.start()
        melt_load.wait()

    def melt(t, field):
        for l in range(LEAD):
            j = jnp.minimum(2 * t + l, ROUNDS * SHIFT - 1)
            chosen = melt_index[j // SHIFT, lax.rem(j, SHIFT)]
            zero = jnp.zeros((rows, cols), jnp.float32)
            for a in range(3):
                field[2 * t + block + l, a, pl.ds(low, rows)] = zero
            for k in range(2):
                value = zero + table[k, 0]
                for e in range(1, table.shape[1]):
                    value = jnp.where(chosen == e, table[k, e], value)
                field[2 * t + block + l, 3 + k, pl.ds(low, rows)] = value

    def arrive(t):
        @pl.when(p < peers - 1)
        def _():
            for l in range(LEAD):
                down_copy(t, l, even).wait_recv()

        for parity, field in ((0, even), (1, odd)):
            @pl.when((p == peers - 1) & (lax.rem(t, 2) == parity))
            def _():
                melt(t, field)

            @pl.when(lax.rem(t, 2) == parity)
            def _():
                for copy in side_copies(t, field):
                    copy.start()

    def sides_done(t):
        for parity, field in ((0, even), (1, odd)):
            @pl.when(lax.rem(t, 2) == parity)
            def _():
                for copy in side_copies(t, field):
                    copy.wait()

    gr = [[DT * grad[a, i] for i in range(3)] for a in range(4)]
    mid = [DT - 2.0 * (gr[a][0] + gr[a][1] + gr[a][2]) for a in range(4)]
    mid = [mid[a] + 1.0 for a in range(4)]
    cm = [0.25 * (comp[k, 0] + comp[k, 1] + comp[k, 2] + comp[k, 3]) for k in range(2)]
    beta = [[DT * (cm[k] - comp[k, a]) for k in range(2)] for a in range(3)]
    lm = 0.25 * (latent[0] + latent[1] + latent[2] + latent[3])
    gl = [DT * (lm - latent[a]) for a in range(3)]
    kd = [DT * diff[k] for k in range(2)]
    km = [1.0 - 6.0 * kd[k] for k in range(2)]
    rel = [[comp[k, a] - comp[k, 3] for k in range(2)] for a in range(3)]
    flat3 = 2.0 * (gr[3][0] + gr[3][1] + gr[3][2]) + mid[3]

    def plane_step(s, j, source, target, edge):
        m = p * block + j
        turn = (s - 1) // STEPS
        top = planes - 1 + SHIFT * turn
        bottom = SHIFT * turn
        cen = j
        up = jnp.where(m == top, j, j + 1)
        down = jnp.where(m == bottom, j, j - 1)
        theta = (m.astype(jnp.float32) - 0.5 * planes) * (1.0 / planes)
        shift = [gl[a] * theta - 0.25 * flat3 + 0.25 for a in range(3)]

        def tile(at):
            here = pl.ds(at, HIGH)
            ctr, gs, xs, ys = [], [], [], []
            for f in range(FIELDS):
                c = source[cen, f, here]
                ctr.append(c)
                gs.append(source[up, f, here] + source[down, f, here])
                xs.append(source[cen, f, pl.ds(at - 1, HIGH)] + source[cen, f, pl.ds(at + 1, HIGH)])
                ys.append(pltpu.roll(c, 1, 1) + pltpu.roll(c, cols - 1, 1))
            w = [
                gr[a][0] * gs[a] + gr[a][1] * xs[a] + gr[a][2] * ys[a] + mid[a] * ctr[a]
                for a in range(3)
            ]
            w3 = (
                gr[3][0] * (gs[0] + gs[1] + gs[2])
                + gr[3][1] * (xs[0] + xs[1] + xs[2])
                + gr[3][2] * (ys[0] + ys[1] + ys[2])
                + mid[3] * (ctr[0] + ctr[1] + ctr[2])
            )
            mean = 0.25 * ((w[0] + w[1]) + (w[2] - w3))
            trial = [
                w[a] - mean + beta[a][0] * ctr[3] + beta[a][1] * ctr[4] + shift[a] for a in range(3)
            ]
            trial.append(1.0 - (trial[0] + trial[1] + trial[2]))
            clipped = [jnp.minimum(jnp.maximum(v, 0.0), 1.0) for v in trial]
            total = (clipped[0] + clipped[1]) + (clipped[2] + clipped[3])
            inv = pl.reciprocal(total, approx=True)
            inv = inv * (2.0 - total * inv)
            fresh = [clipped[a] * inv for a in range(3)]
            change = [fresh[a] - ctr[a] for a in range(3)]
            for k in range(2):
                around = (gs[3 + k] + xs[3 + k]) + ys[3 + k]
                value = km[k] * ctr[3 + k] + kd[k] * around
                fresh.append(value - (
                    rel[0][k] * change[0] + rel[1][k] * change[1] + rel[2][k] * change[2]
                ))
            put(at, HIGH, fresh)

        def put(at, size, fresh):
            if target is None:
                i = j - 2 * TOTAL
                out = pl.ds(at - low, size)
                for a in range(3):
                    phases[a, i, out] = fresh[a]
                phases[3, i, out] = 1.0 - (fresh[0] + fresh[1] + fresh[2])
                for k in range(2):
                    potentials[k, i, out] = fresh[3 + k]
            else:
                for f in range(FIELDS):
                    target[j, f, pl.ds(at, size)] = fresh[f]

        @pl.when(m <= top)
        def _():
            for at in range(PAD + 8 * edge, PAD + 2 * halo + rows - 8 * edge, HIGH):
                tile(at)

        @pl.when(m > top)
        def _():
            size = 2 * halo + rows - 16 * edge
            put(PAD + 8 * edge, size, [source[cen, f, pl.ds(PAD + 8 * edge, size)] for f in range(FIELDS)])

    def group(g, level):
        first = 2 * level + GROUP * g
        last = first + GROUP + jnp.where(g == GROUPS - 1, block - GROUP * GROUPS, 0)

        lowest = first + jnp.where(g == 0, 2, 0)

        def run(source, target, edge, begin, end):
            def one(j, c):
                plane_step(level, j, source, target, edge)
                return c

            lax.fori_loop(begin, end, one, 0)

        for parity, source, target in ((1, even, odd), (0, odd, even)):
            @pl.when((lax.rem(level, 2) == parity) & (level < TOTAL))
            def _():
                run(source, target, 1, first, lowest)
                run(source, target, 0, lowest, last)

        @pl.when(level == TOTAL)
        def _():
            run(odd, None, 1, first, last)

            def write(j, c):
                for copy in stores(j - 2 * TOTAL):
                    copy.start()
                return c

            lax.fori_loop(first, last, write, 0)

    def iteration(n, carry):
        @pl.when((n >= GROUPS - 1) & (n - GROUPS + 1 < TOTAL))
        def _():
            arrive(n - GROUPS + 1)

        def descend(k, c):
            g = GROUPS - 1 - k
            level = n - g

            @pl.when((g == GROUPS - 1) & (level >= 1))
            def _():
                sides_done(level - 1)

            @pl.when(level == 1)
            def _():
                for c in range(4):
                    @pl.when(g == max(c - 1, 0))
                    def _():
                        for copy in own_copies(c):
                            copy.wait()

            @pl.when((level >= 1) & (level <= TOTAL))
            def _():
                group(g, level)

            for parity, field in ((0, even), (1, odd)):
                @pl.when(
                    helps & (k == HELP_AT) & (n >= 2) & (n - 2 < TOTAL) & (lax.rem(n, 2) == parity)
                )
                def _():
                    help_down(n - 2, parity, field)

            return c

        lax.fori_loop(0, GROUPS, descend, 0)

        for parity, field in ((0, even), (1, odd)):
            @pl.when((n < TOTAL) & (lax.rem(n, 2) == parity))
            def _():
                send_down(n, parity, field)

        return carry

    lax.fori_loop(1, TOTAL + GROUPS, iteration, 0)

    def written(i, carry):
        for copy in stores(i):
            copy.wait()
        return carry

    lax.fori_loop(0, block, written, 0)

    @pl.when(p > 0)
    def _():
        def sent(t, carry):
            for l in range(LEAD):
                down_copy(t, l, even).wait_send()
            return carry

        lax.fori_loop(0, TOTAL, sent, 0)

    @pl.when(helps)
    def _():
        def helped(h, carry):
            for parity, field in ((0, even), (1, odd)):
                for l in range(parity + 1):
                    help_copy(2 * h + parity, l, field).wait_send()
            return carry

        lax.fori_loop(0, TOTAL // 2, helped, 0)


def solution(mesh):
    peers, lats = mesh.shape["grow"], mesh.shape["lat"]

    def on_device(labels, rough, pot, grad, comp, latent, diff, table, melt_index):
        block, rows, cols = labels.shape
        span = block + 2 * TOTAL + LEAD
        field = pltpu.VMEM((span, FIELDS, rows + 2 * HALO + 2 * PAD, cols), jnp.float32)
        hbm = pl.BlockSpec(memory_space=pltpu.HBM)
        smem = pl.BlockSpec(memory_space=pltpu.SMEM)
        return pl.pallas_call(
            functools.partial(kernel, peers, lats),
            out_shape=(
                jax.ShapeDtypeStruct((4, block, rows, cols), jnp.float32),
                jax.ShapeDtypeStruct((2, block, rows, cols), jnp.float32),
            ),
            in_specs=[hbm] * 4 + [smem] * 5,
            out_specs=(hbm, hbm),
            scratch_shapes=[field, field] + [
                pltpu.SemaphoreType.DMA((TOTAL, LEAD)),
                pltpu.SemaphoreType.DMA((TOTAL, LEAD)),
                pltpu.SemaphoreType.DMA((TOTAL, 2)),
                pltpu.SemaphoreType.DMA((TOTAL, 2)),
                pltpu.SemaphoreType.DMA((4, 2)),
                pltpu.SemaphoreType.DMA((4, 2)),
                pltpu.VMEM((TOTAL, 2, FIELDS, rows, cols), jnp.float32),
                pltpu.SemaphoreType.DMA((TOTAL, 2)),
                pltpu.SemaphoreType.DMA((TOTAL, 2)),
                pltpu.VMEM((block, rows, cols), jnp.int32),
                pltpu.VMEM((4, block, rows, cols), jnp.float32),
                pltpu.VMEM((2, block, rows, cols), jnp.float32),
                pltpu.VMEM((ROUNDS, SHIFT, rows, cols), jnp.int32),
                pltpu.SemaphoreType.DMA((13,)),
                pltpu.VMEM((4, block, rows, cols), jnp.float32),
                pltpu.VMEM((2, block, rows, cols), jnp.float32),
                pltpu.SemaphoreType.DMA((block, 2)),
            ],
            compiler_params=pltpu.CompilerParams(
                collective_id=0, has_side_effects=True, vmem_limit_bytes=60 << 20
            ),
        )(labels, rough, pot, melt_index, grad, comp.T, latent, diff, table.T)

    placed = (
        P("grow", "lat", None),
        P(None, "grow", "lat", None),
        P(None, "grow", "lat", None),
        P(),
        P(),
        P(),
        P(),
        P(),
        P(None, None, "lat", None),
    )
    return jax.shard_map(
        on_device,
        mesh=mesh,
        in_specs=placed,
        out_specs=(P(None, "grow", "lat", None), P(None, "grow", "lat", None)),
        check_vma=False,
    )
```

```python
import functools

import jax
import jax.numpy as jnp
from jax import lax
from jax.experimental import pallas as pl
from jax.experimental.pallas import tpu as pltpu
from jax.sharding import PartitionSpec as P

MESH = pl.DeviceIdType.MESH
STEPS = 4
ROUNDS = 4
SHIFT = 8
DT = 0.04
TOTAL = STEPS * ROUNDS
FIELDS = 5
PAD = 8
LEAD = 3
LINE = 8
HALO = 8
HELP_AT = 3
GROUP = 3
GROUPS = 5
HIGH = 16


def kernel(
    peers,
    lats,
    labels_in,
    rough_in,
    pot_in,
    melt_in,
    grad,
    comp,
    latent,
    diff,
    table,
    phases_out,
    potentials_out,
    odd,
    even,
    z_send,
    z_recv,
    x_send,
    x_recv,
    own_send,
    own_recv,
    detour,
    d_send,
    d_recv,
    labels,
    rough,
    pot,
    melt_index,
    load,
    phases,
    potentials,
    store,
):
    block, rows, cols = labels.shape
    halo = HALO
    low = PAD + halo
    high = low + rows
    planes = peers * block
    p = lax.axis_index("grow")
    q = lax.axis_index("lat")
    below = jnp.maximum(p - 1, 0)
    above = jnp.minimum(p + 1, peers - 1)
    z = lax.rem(p, LINE)
    turns = (z == 0) & (p >= LINE)
    helps = (z == 0) & (p < peers - LINE)
    left = lax.rem(q + lats - 1, lats)
    right = lax.rem(q + 1, lats)

    def loads(c):
        some = pl.ds(4 * c, 4)
        return (
            pltpu.make_async_copy(labels_in.at[some], labels.at[some], load.at[3 * c]),
            pltpu.make_async_copy(rough_in.at[:, some], rough.at[:, some], load.at[3 * c + 1]),
            pltpu.make_async_copy(pot_in.at[:, some], pot.at[:, some], load.at[3 * c + 2]),
        )

    melt_load = pltpu.make_async_copy(melt_in, melt_index, load.at[12])
    barrier = pltpu.get_barrier_semaphore()
    for side in (left, right):
        pl.semaphore_signal(barrier, inc=1, device_id=(p, side), device_id_type=MESH)

    @pl.when(p < peers - 1)
    def _():
        pl.semaphore_signal(barrier, inc=1, device_id=(above, q), device_id_type=MESH)

    @pl.when(helps)
    def _():
        pl.semaphore_signal(
            barrier, inc=1, device_id=(jnp.minimum(p + LINE, peers - 1), q), device_id_type=MESH
        )

    @pl.when((z == LINE - 1) & (p < peers - 1))
    def _():
        pl.semaphore_signal(
            barrier, inc=1, device_id=(jnp.maximum(p - LINE + 1, 0), q), device_id_type=MESH
        )

    for c in range(4):
        for copy in loads(c):
            copy.start()

    def stores(i):
        return (
            pltpu.make_async_copy(phases.at[:, i], phases_out.at[:, i], store.at[i, 0]),
            pltpu.make_async_copy(potentials.at[:, i], potentials_out.at[:, i], store.at[i, 1]),
        )

    def begin(i, carry):
        label = labels[i]
        parts = [rough[a, i] for a in range(4)]
        scale = 1.0 / (3.0 + (parts[0] + parts[1] + parts[2] + parts[3]))
        for a in range(3):
            even[i, a, pl.ds(low, rows)] = (jnp.where(label == a, 3.0, 0.0) + parts[a]) * scale
        for k in range(2):
            even[i, 3 + k, pl.ds(low, rows)] = pot[k, i]
        return carry

    def start_part(c):
        for copy in loads(c):
            copy.wait()
        lax.fori_loop(4 * c, 4 * c + 4, begin, 0)

    start_part(0)
    pl.semaphore_wait(
        barrier,
        2 + (p > 0).astype(jnp.int32) + turns.astype(jnp.int32) + helps.astype(jnp.int32),
    )

    def lands(t, l, field):
        return field.at[2 * t + block + l, :, pl.ds(low, rows)]

    def down_copy(t, l, field):
        return pltpu.make_async_remote_copy(
            field.at[2 * t + l, :, pl.ds(low, rows)],
            lands(t, l, field),
            z_send.at[t, l],
            z_recv.at[t, l],
            device_id=(below, q),
            device_id_type=MESH,
        )

    def turn_copy(t, l, field):
        return pltpu.make_async_remote_copy(
            field.at[2 * t + l, :, pl.ds(low, rows)],
            detour.at[t, l],
            z_send.at[t, l],
            d_recv.at[t, l],
            device_id=(jnp.maximum(p - LINE, 0), q),
            device_id_type=MESH,
        )

    def help_copy(t, l, field):
        return pltpu.make_async_remote_copy(
            detour.at[t, l],
            lands(t, l, field),
            d_send.at[t, l],
            z_recv.at[t, l],
            device_id=(jnp.minimum(p + LINE - 1, peers - 1), q),
            device_id_type=MESH,
        )

    def send_down(t, parity, field):
        @pl.when(turns)
        def _():
            for l in range(LEAD):
                (turn_copy if l <= parity else down_copy)(t, l, field).start()

        @pl.when((p > 0) & (z > 0))
        def _():
            for l in range(LEAD):
                down_copy(t, l, field).start()

    def help_down(t, parity, field):
        for l in range(parity + 1):
            turn_copy(t, l, field).wait_recv()
            help_copy(t, l, field).start()

    def halo_copies(field, at, count, send, recv):
        return (
            pltpu.make_async_remote_copy(
                field.at[pl.ds(at, count), :, pl.ds(low, halo)],
                field.at[pl.ds(at, count), :, pl.ds(high, halo)],
                send.at[0], recv.at[0],
                device_id=(p, left), device_id_type=MESH,
            ),
            pltpu.make_async_remote_copy(
                field.at[pl.ds(at, count), :, pl.ds(high - halo, halo)],
                field.at[pl.ds(at, count), :, pl.ds(low - halo, halo)],
                send.at[1], recv.at[1],
                device_id=(p, right), device_id_type=MESH,
            ),
        )

    def own_copies(c):
        return halo_copies(even, 4 * c, 4, own_send.at[c], own_recv.at[c])

    def side_copies(t, field, count):
        return halo_copies(field, 2 * t + block, count, x_send.at[t], x_recv.at[t])

    send_down(0, 0, even)

    for c in range(4):
        if c > 0:
            start_part(c)
        for copy in own_copies(c):
            copy.start()

    @pl.when(p == peers - 1)
    def _():
        melt_load.start()
        melt_load.wait()

    def melt(t, field):
        for l in range(LEAD):
            j = jnp.minimum(2 * t + l, ROUNDS * SHIFT - 1)
            chosen = melt_index[j // SHIFT, lax.rem(j, SHIFT)]
            zero = jnp.zeros((rows, cols), jnp.float32)
            for a in range(3):
                field[2 * t + block + l, a, pl.ds(low, rows)] = zero
            for k in range(2):
                value = zero + table[k, 0]
                for e in range(1, table.shape[1]):
                    value = jnp.where(chosen == e, table[k, e], value)
                field[2 * t + block + l, 3 + k, pl.ds(low, rows)] = value

    def landed(t, l):
        @pl.when(p < peers - 1)
        def _():
            down_copy(t, l, even).wait_recv()

    def arrive(t):
        for parity, field in ((0, even), (1, odd)):
            @pl.when((p == peers - 1) & (lax.rem(t, 2) == parity))
            def _():
                melt(t, field)

        landed(t, 0)
        landed(t, 1)

        @pl.when(t == TOTAL - 1)
        def _():
            for copy in side_copies(t, odd, LEAD - 1):
                copy.start()

        landed(t, 2)
        for parity, field in ((0, even), (1, odd)):
            @pl.when((t < TOTAL - 1) & (lax.rem(t, 2) == parity))
            def _():
                for copy in side_copies(t, field, LEAD):
                    copy.start()

    def sides_done(t):
        @pl.when(t == TOTAL - 1)
        def _():
            for copy in side_copies(t, odd, LEAD - 1):
                copy.wait()

        for parity, field in ((0, even), (1, odd)):
            @pl.when((t < TOTAL - 1) & (lax.rem(t, 2) == parity))
            def _():
                for copy in side_copies(t, field, LEAD):
                    copy.wait()

    gr = [[DT * grad[a, i] for i in range(3)] for a in range(4)]
    mid = [DT - 2.0 * (gr[a][0] + gr[a][1] + gr[a][2]) for a in range(4)]
    mid = [mid[a] + 1.0 for a in range(4)]
    cm = [0.25 * (comp[k, 0] + comp[k, 1] + comp[k, 2] + comp[k, 3]) for k in range(2)]
    beta = [[DT * (cm[k] - comp[k, a]) for k in range(2)] for a in range(3)]
    lm = 0.25 * (latent[0] + latent[1] + latent[2] + latent[3])
    gl = [DT * (lm - latent[a]) for a in range(3)]
    kd = [DT * diff[k] for k in range(2)]
    km = [1.0 - 6.0 * kd[k] for k in range(2)]
    rel = [[comp[k, a] - comp[k, 3] for k in range(2)] for a in range(3)]
    flat3 = 2.0 * (gr[3][0] + gr[3][1] + gr[3][2]) + mid[3]

    def plane_step(s, j, source, target, edge):
        m = p * block + j
        turn = (s - 1) // STEPS
        top = planes - 1 + SHIFT * turn
        bottom = SHIFT * turn
        cen = j
        up = jnp.where(m == top, j, j + 1)
        down = jnp.where(m == bottom, j, j - 1)
        theta = (m.astype(jnp.float32) - 0.5 * planes) * (1.0 / planes)
        shift = [gl[a] * theta - 0.25 * flat3 + 0.25 for a in range(3)]

        def tile(at):
            here = pl.ds(at, HIGH)
            ctr, gs, xs, ys = [], [], [], []
            for f in range(FIELDS):
                c = source[cen, f, here]
                ctr.append(c)
                gs.append(source[up, f, here] + source[down, f, here])
                xs.append(source[cen, f, pl.ds(at - 1, HIGH)] + source[cen, f, pl.ds(at + 1, HIGH)])
                ys.append(pltpu.roll(c, 1, 1) + pltpu.roll(c, cols - 1, 1))
            w = [
                gr[a][0] * gs[a] + gr[a][1] * xs[a] + gr[a][2] * ys[a] + mid[a] * ctr[a]
                for a in range(3)
            ]
            w3 = (
                gr[3][0] * (gs[0] + gs[1] + gs[2])
                + gr[3][1] * (xs[0] + xs[1] + xs[2])
                + gr[3][2] * (ys[0] + ys[1] + ys[2])
                + mid[3] * (ctr[0] + ctr[1] + ctr[2])
            )
            mean = 0.25 * ((w[0] + w[1]) + (w[2] - w3))
            trial = [
                w[a] - mean + beta[a][0] * ctr[3] + beta[a][1] * ctr[4] + shift[a] for a in range(3)
            ]
            trial.append(1.0 - (trial[0] + trial[1] + trial[2]))
            clipped = [jnp.minimum(jnp.maximum(v, 0.0), 1.0) for v in trial]
            total = (clipped[0] + clipped[1]) + (clipped[2] + clipped[3])
            inv = pl.reciprocal(total, approx=True)
            inv = inv * (2.0 - total * inv)
            fresh = [clipped[a] * inv for a in range(3)]
            change = [fresh[a] - ctr[a] for a in range(3)]
            for k in range(2):
                around = (gs[3 + k] + xs[3 + k]) + ys[3 + k]
                value = km[k] * ctr[3 + k] + kd[k] * around
                fresh.append(value - (
                    rel[0][k] * change[0] + rel[1][k] * change[1] + rel[2][k] * change[2]
                ))
            put(at, HIGH, fresh)

        def put(at, size, fresh):
            if target is None:
                i = j - 2 * TOTAL
                out = pl.ds(at - low, size)
                for a in range(3):
                    phases[a, i, out] = fresh[a]
                phases[3, i, out] = 1.0 - (fresh[0] + fresh[1] + fresh[2])
                for k in range(2):
                    potentials[k, i, out] = fresh[3 + k]
            else:
                for f in range(FIELDS):
                    target[j, f, pl.ds(at, size)] = fresh[f]

        @pl.when(m <= top)
        def _():
            for at in range(PAD + 8 * edge, PAD + 2 * halo + rows - 8 * edge, HIGH):
                tile(at)

        @pl.when(m > top)
        def _():
            size = 2 * halo + rows - 16 * edge
            put(PAD + 8 * edge, size, [source[cen, f, pl.ds(PAD + 8 * edge, size)] for f in range(FIELDS)])

    def group(g, level):
        first = 2 * level + GROUP * g
        last = first + GROUP + jnp.where(g == GROUPS - 1, block - GROUP * GROUPS, 0)

        lowest = first + jnp.where(g == 0, 2, 0)

        def run(source, target, edge, begin, end):
            def one(j, c):
                plane_step(level, j, source, target, edge)
                return c

            lax.fori_loop(begin, end, one, 0)

        for parity, source, target in ((1, even, odd), (0, odd, even)):
            @pl.when((lax.rem(level, 2) == parity) & (level < TOTAL))
            def _():
                run(source, target, 1, first, lowest)
                run(source, target, 0, lowest, last)

        @pl.when(level == TOTAL)
        def _():
            run(odd, None, 1, first, last)

            def write(j, c):
                for copy in stores(j - 2 * TOTAL):
                    copy.start()
                return c

            lax.fori_loop(first, last, write, 0)

    def iteration(n, carry):
        @pl.when((n >= GROUPS - 1) & (n - GROUPS + 1 < TOTAL))
        def _():
            arrive(n - GROUPS + 1)

        def descend(k, c):
            g = GROUPS - 1 - k
            level = n - g

            @pl.when((g == GROUPS - 1) & (level >= 1))
            def _():
                sides_done(level - 1)

            @pl.when(level == 1)
            def _():
                for c in range(4):
                    @pl.when(g == max(c - 1, 0))
                    def _():
                        for copy in own_copies(c):
                            copy.wait()

            @pl.when((level >= 1) & (level <= TOTAL))
            def _():
                group(g, level)

            for parity, field in ((0, even), (1, odd)):
                @pl.when(
                    helps & (k == HELP_AT) & (n >= 2) & (n - 2 < TOTAL) & (lax.rem(n, 2) == parity)
                )
                def _():
                    help_down(n - 2, parity, field)

            return c

        lax.fori_loop(0, GROUPS, descend, 0)

        for parity, field in ((0, even), (1, odd)):
            @pl.when((n < TOTAL) & (lax.rem(n, 2) == parity))
            def _():
                send_down(n, parity, field)

        return carry

    lax.fori_loop(1, TOTAL + GROUPS, iteration, 0)

    def written(i, carry):
        for copy in stores(i):
            copy.wait()
        return carry

    lax.fori_loop(0, block, written, 0)

    @pl.when(p > 0)
    def _():
        def sent(t, carry):
            for l in range(LEAD):
                down_copy(t, l, even).wait_send()
            return carry

        lax.fori_loop(0, TOTAL, sent, 0)

    @pl.when(helps)
    def _():
        def helped(h, carry):
            for parity, field in ((0, even), (1, odd)):
                for l in range(parity + 1):
                    help_copy(2 * h + parity, l, field).wait_send()
            return carry

        lax.fori_loop(0, TOTAL // 2, helped, 0)


def solution(mesh):
    peers, lats = mesh.shape["grow"], mesh.shape["lat"]

    def on_device(labels, rough, pot, grad, comp, latent, diff, table, melt_index):
        block, rows, cols = labels.shape
        span = block + 2 * TOTAL + LEAD
        field = pltpu.VMEM((span, FIELDS, rows + 2 * HALO + 2 * PAD, cols), jnp.float32)
        hbm = pl.BlockSpec(memory_space=pltpu.HBM)
        smem = pl.BlockSpec(memory_space=pltpu.SMEM)
        return pl.pallas_call(
            functools.partial(kernel, peers, lats),
            out_shape=(
                jax.ShapeDtypeStruct((4, block, rows, cols), jnp.float32),
                jax.ShapeDtypeStruct((2, block, rows, cols), jnp.float32),
            ),
            in_specs=[hbm] * 4 + [smem] * 5,
            out_specs=(hbm, hbm),
            scratch_shapes=[field, field] + [
                pltpu.SemaphoreType.DMA((TOTAL, LEAD)),
                pltpu.SemaphoreType.DMA((TOTAL, LEAD)),
                pltpu.SemaphoreType.DMA((TOTAL, 2)),
                pltpu.SemaphoreType.DMA((TOTAL, 2)),
                pltpu.SemaphoreType.DMA((4, 2)),
                pltpu.SemaphoreType.DMA((4, 2)),
                pltpu.VMEM((TOTAL, 2, FIELDS, rows, cols), jnp.float32),
                pltpu.SemaphoreType.DMA((TOTAL, 2)),
                pltpu.SemaphoreType.DMA((TOTAL, 2)),
                pltpu.VMEM((block, rows, cols), jnp.int32),
                pltpu.VMEM((4, block, rows, cols), jnp.float32),
                pltpu.VMEM((2, block, rows, cols), jnp.float32),
                pltpu.VMEM((ROUNDS, SHIFT, rows, cols), jnp.int32),
                pltpu.SemaphoreType.DMA((13,)),
                pltpu.VMEM((4, block, rows, cols), jnp.float32),
                pltpu.VMEM((2, block, rows, cols), jnp.float32),
                pltpu.SemaphoreType.DMA((block, 2)),
            ],
            compiler_params=pltpu.CompilerParams(
                collective_id=0, has_side_effects=True, vmem_limit_bytes=60 << 20
            ),
        )(labels, rough, pot, melt_index, grad, comp.T, latent, diff, table.T)

    placed = (
        P("grow", "lat", None),
        P(None, "grow", "lat", None),
        P(None, "grow", "lat", None),
        P(),
        P(),
        P(),
        P(),
        P(),
        P(None, None, "lat", None),
    )
    return jax.shard_map(
        on_device,
        mesh=mesh,
        in_specs=placed,
        out_specs=(P(None, "grow", "lat", None), P(None, "grow", "lat", None)),
        check_vma=False,
    )
```
